256 devices in a mesh: replica: 8 (over y_lo, x), fsdp: 32 (over y_hi, z, core).
Axes of the slice: x: 4, y: 4 (y_hi: 2, y_lo: 2; y = y_hi * 2 + y_lo), z: 8, core: 2. Of those that a mesh axis runs over, the one named last changes fastest.
Arguments:
- hidden: bfloat16 [65536, 10240], P(('replica', 'fsdp')), may hold values from -6 to 6
- norm_gain: float32 [10240], replicated, may hold values from 0.5 to 1.5
- local_weight: bfloat16 [8, 10240, 1024], P('replica', 'fsdp'), may hold values from -6 to 6
- global_weight: float32 [10240, 1024], P('fsdp'), may hold values from -6 to 6
- momentum: float32 [10240, 1024], P('fsdp'), may hold values from -4 to 4
Outputs:
- keys: bfloat16 [65536, 1024], P(('replica', 'fsdp'))
- new_global: float32 [10240, 1024], P('fsdp')
- new_momentum: float32 [10240, 1024], P('fsdp')
The draws below stay inside these ranges and needn't reach their ends.
All inputs are finite; a program needn't handle non-finite values.
Results may differ from the reference program's by a relative error of at most 0.019.
Values may be sent and summed in bfloat16 or wider, within the bound.
A program may use at most 128 MiB of HBM per device.

```python
import math
import jax
import jax.numpy as jnp
from jax import lax

D = 10240
KV = 1024
BLOCK = 128
TOK_DEV = 256
TOKENS = 65536
N_REPLICA = 8
N_FSDP = 32


def block_levels(stream_key, shape, pieces, smallest, high):
    factor_of, own = 1.0, jax.random.fold_in(stream_key, 6)
    for position, parts in pieces:
        heights = jnp.exp(jax.random.uniform(jax.random.fold_in(own, position), (parts,), jnp.float32, smallest / len(pieces), high / len(pieces)))
        factor_of = factor_of * jnp.repeat(heights, shape[position] // parts).reshape([-1 if axis == position else 1 for axis in range(len(shape))])
    return factor_of


def centred(rng, shape, width, bound, cuts=(), held_as=jnp.bfloat16):
    array = jax.random.normal(rng, shape, jnp.float32) * width
    if len(cuts) > 0:
        array = block_levels(rng, shape, cuts, -0.22, 0.18) * array
    return jnp.clip(array, min=-bound, max=bound).astype(held_as)


def setup_inputs(seed: int = 0) -> dict:
    seeds = jax.random.split(jax.random.key(seed), 6)
    hidden = centred(seeds[0], (TOKENS, D), 1.0, 6.0, ((0, 256),))
    norm_gain = jnp.clip(1.0 + 0.1 * jax.random.normal(seeds[1], (D,), jnp.float32), 0.5, 1.5)
    local_weight = centred(seeds[2], (N_REPLICA, D, KV), 1.0, 6.0, ((0, 8), (1, 32)))
    global_weight = centred(seeds[3], (D, KV), 1.0, 6.0, ((0, 32),), jnp.float32)
    momentum = centred(seeds[4], (D, KV), 0.5, 4.0, ((0, 32),), jnp.float32)
    return dict(hidden=hidden, norm_gain=norm_gain, local_weight=local_weight, global_weight=global_weight, momentum=momentum)


def normed_rows(block_rows, norm_gain):
    floats = block_rows.astype(jnp.float32)
    inverse = lax.rsqrt(lax.optimization_barrier(jnp.mean(floats * floats, axis=-1, keepdims=True)) + 1e-05)
    return (floats * inverse * norm_gain).astype(jnp.bfloat16)

def reference(hidden, norm_gain, local_weight, global_weight, momentum):
    factor = 1.0 / math.sqrt(D)
    grouped = hidden.reshape(N_REPLICA, TOK_DEV * N_FSDP, D)

    def replica_keys(pair):
        rows, weight = pair
        normed = normed_rows(rows, norm_gain)
        return (jnp.dot(normed, weight, preferred_element_type=jnp.float32) * factor).astype(jnp.bfloat16)
    keys = lax.map(replica_keys, (grouped, local_weight)).reshape(TOKENS, KV)
    delta = global_weight[None] - local_weight.astype(jnp.float32)
    blocks = delta.reshape(N_REPLICA, D, KV // BLOCK, BLOCK)
    scale = (lax.optimization_barrier(jnp.max(jnp.abs(blocks), axis=-1)) + 1e-06).astype(jnp.bfloat16)
    wide_scale = scale[..., None].astype(jnp.float32)
    code = (blocks / wide_scale).astype(jnp.bfloat16)
    decoded = code.astype(jnp.float32) * wide_scale
    mean_delta = (lax.optimization_barrier(jnp.sum(decoded, axis=0)) / N_REPLICA).reshape(D, KV)
    new_momentum = 0.9 * momentum + mean_delta
    new_global = global_weight - 0.7 * (0.9 * new_momentum + mean_delta)
    return (keys, new_global, new_momentum)
```

```python
import functools
import math

import jax
import jax.numpy as jnp
from jax import lax
from jax.experimental import pallas as pl
from jax.experimental.pallas import tpu as pltpu
from jax.sharding import PartitionSpec as P

MESH = pl.DeviceIdType.MESH
BLOCK = 128
F32 = jnp.float32
BF16 = jnp.bfloat16

RING = (
    ("B", 0, 0), ("B", 1, 0), ("B", 0, 1), ("B", 1, 1), ("A", 0, 0), ("A", 1, 0), ("B", 0, 2),
    ("B", 1, 2), ("B", 0, 3), ("A", 0, 1), ("A", 1, 1), ("A", 0, 2), ("A", 1, 2), ("A", 0, 3),
)
N_RING = len(RING)


def kernel(
    ws, hid, wl_in, g_in, m_in, keys_out, ng_out, nm_out,
    H, HP, WB, WX, acc, PS, PR, wl, gl, mo, dec, rsb, ysend, yrecv, mean, ng, nm, inv, KO, KS,
    loc, sib_s, sib_r, rel_s, rel_r, z_s, z_r, yc_s, yc_r, yh_s, yh_r, yp_s, yp_r, x_s, x_r, xg_s, xg_r, yl_s, yl_r,
):
    replica, fsdp = lax.axis_index("replica"), lax.axis_index("fsdp")
    x, ylo = lax.rem(replica, 4), lax.div(replica, 4)
    c, z, r = lax.rem(fsdp, 2), lax.rem(lax.div(fsdp, 2), 8), lax.div(fsdp, 16)
    o = 1 - c

    def at_fsdp(r_, z_, c_):
        return (replica, r_ * 16 + z_ * 2 + c_)

    sib = at_fsdp(r, z, o)
    zdev = (at_fsdp(r, lax.rem(z + 1, 8), c), at_fsdp(r, lax.rem(z + 7, 8), c))
    partner = at_fsdp(1 - r, z, c)
    xdev = [(ylo * 4 + lax.rem(x + j, 4), fsdp) for j in (1, 2, 3)]
    ydev = ((1 - ylo) * 4 + x, fsdp)

    def remote(src, dst, s, rcv, dev):
        return pltpu.make_async_remote_copy(
            src_ref=src, dst_ref=dst, send_sem=s, recv_sem=rcv, device_id=dev, device_id_type=MESH
        )

    l_h = pltpu.make_async_copy(hid, H.at[pl.ds(pl.multiple_of(c * 256, 256), 256)], loc.at[0])
    own_cols = pl.ds(pl.multiple_of(c * 512, 512), 512)
    oth_cols = pl.ds(pl.multiple_of(o * 512, 512), 512)
    own_rows = pl.ds(pl.multiple_of(c * 320, 64), 320)
    l_w = pltpu.make_async_copy(ws.at[:, own_cols], WB.at[z, own_rows], loc.at[1])
    l_wl = pltpu.make_async_copy(wl_in, wl, loc.at[2])
    l_g = pltpu.make_async_copy(g_in, gl, loc.at[3])
    l_m = pltpu.make_async_copy(m_in, mo, loc.at[4])
    l_w.start()
    l_wl.start()
    l_g.start()
    l_h.start()
    l_m.start()

    barrier = pltpu.get_barrier_semaphore()
    everyone = [sib, zdev[0], zdev[1], partner, ydev] + xdev
    for dev in everyone:
        pl.semaphore_signal(barrier, inc=1, device_id=dev, device_id_type=MESH)
    pl.semaphore_wait(barrier, len(everyone))

    w_sib = remote(ws.at[:, oth_cols], WB.at[z, own_rows], sib_s.at[0], sib_r.at[0], sib)
    w_sib.start()

    def hid_group(q):
        g, half = divmod(q, 2)
        out = []
        for zb in range(half * 4, half * 4 + 4):
            col = pl.multiple_of((1 - r) * 5120 + zb * 640, 128)
            out.append(remote(
                hid.at[pl.ds(g * 128, 128), pl.ds(col, 512)],
                HP.at[g, pl.ds(pl.multiple_of(c * 128, 128), 128), pl.ds(zb * 512, 512)],
                yh_s.at[q, zb % 4], yh_r.at[q, zb % 4], partner,
            ))
        return out

    def relay(q):
        g, half = divmod(q, 2)
        part = HP.at[g, pl.ds(pl.multiple_of(c * 128, 128), 128), pl.ds(half * 2048, 2048)]
        return remote(part, part, rel_s.at[q], rel_r.at[q], sib)

    groups = [hid_group(q) for q in range(4)]
    relays = [relay(q) for q in range(4)]

    def chunk_ref(kind, half, slot):
        if kind == "B":
            return WB.at[slot, pl.ds(half * 256, 256)]
        if half == 0:
            return WB.at[slot, pl.ds(512, 128)]
        return WX.at[slot]

    def slot_of(way, dist):
        return lax.rem(z + (8 - dist if way == 0 else dist), 8)

    def ring_copy(way, i):
        kind, half, dist = RING[i]
        part = chunk_ref(kind, half if way == 0 else 1 - half, slot_of(way, dist))
        return remote(part, part, z_s.at[way, i], z_r.at[way, i], zdev[way])

    ring = [[ring_copy(way, i) for i in range(N_RING)] for way in range(2)]

    l_w.wait()
    w_sib.wait_recv()
    for i in range(2):
        for way in range(2):
            ring[way][i].start()
    cross = remote(WB.at[z, pl.ds(512, 128)], WX.at[z], yc_s, yc_r, partner)
    cross.start()
    for cp in groups[0]:
        cp.start()
    h_sib = remote(
        hid, H.at[pl.ds(pl.multiple_of(c * 256, 256), 256)], sib_s.at[1], sib_r.at[1], sib
    )
    h_sib.start()
    for cp in groups[1]:
        cp.start()

    l_wl.wait()
    l_g.wait()

    @pl.loop(0, 20)
    def _(i):
        rows = pl.ds(pl.multiple_of(i * 16, 16), 16)
        for b in range(8):
            cols = pl.ds(b * BLOCK, BLOCK)
            d = gl[rows, cols] - wl[rows, cols].astype(F32)
            s = (jnp.max(jnp.abs(d), axis=-1, keepdims=True) + 1e-06).astype(BF16).astype(F32)
            dec[rows, cols] = (d / s).astype(BF16).astype(F32) * s

    def quarter(q):
        return pl.ds(pl.multiple_of(q * 80, 16), 80)

    scatter = [
        remote(dec.at[quarter(lax.rem(x + j, 4))], rsb.at[j - 1], x_s.at[j - 1], x_r.at[j - 1], xdev[j - 1])
        for j in (1, 2, 3)
    ]
    for cp in scatter:
        cp.start()
    ysum = remote(ysend, yrecv, yl_s, yl_r, ydev)
    spread = [
        remote(mean.at[quarter(x)], mean.at[quarter(x)], xg_s.at[j - 1], xg_r.at[j - 1], xdev[j - 1])
        for j in (1, 2, 3)
    ]
    acc[...] = jnp.zeros_like(acc)

    def mm(h_col, w_ref, depth):
        for n in range(2):
            cols = pl.ds(n * 256, 256)
            acc[:, cols] += jnp.dot(
                H[:, pl.ds(pl.multiple_of(h_col, 128), depth)], w_ref[:, cols], preferred_element_type=F32
            )

    def mm_chunk(kind, half, slot):
        base = slot * 640
        if kind == "B":
            mm(r * 5120 + base + half * 256, chunk_ref(kind, half, slot), 256)
        elif half == 0:
            mm(r * 5120 + base + 512, chunk_ref(kind, half, slot), 128)
        else:
            mm((1 - r) * 5120 + base + 512, chunk_ref(kind, half, slot), 128)

    def mm_arrival(i):
        kind, half, dist = RING[i]
        if kind == "B":
            @pl.loop(0, 2)
            def _(way):
                slot = lax.rem(z + 8 + (2 * way - 1) * (dist + 1), 8)
                h_ = way if half == 0 else 1 - way
                mm(
                    r * 5120 + slot * 640 + h_ * 256,
                    WB.at[slot, pl.ds(pl.multiple_of(h_ * 256, 256), 256)], 256,
                )
        else:
            for way in range(2):
                mm_chunk(kind, half if way == 0 else 1 - half, slot_of(way, dist + 1))

    def mean_squares(part):
        @pl.loop(0, 4)
        def _(i):
            rows = pl.ds(pl.multiple_of(part * 256 + i * 64, 64), 64)

            def body(k, total):
                for s in range(4):
                    v = H[rows, pl.ds(pl.multiple_of(k * 512 + s * 128, 128), 128)].astype(F32)
                    total = total + v * v
                return total

            total = lax.fori_loop(0, 20, body, jnp.zeros((64, 128), F32))
            ms = jnp.sum(total, axis=-1, keepdims=True) * (1.0 / 10240)
            inv[rows, :] = jnp.broadcast_to(lax.rsqrt(ms + 1e-05) * (1.0 / math.sqrt(10240)), (64, 128))

    def partner_sums(g):
        for n in range(2):
            cols = pl.ds(n * 256, 256)

            def body(s, total):
                return total + jnp.dot(
                    HP[g, :, pl.ds(pl.multiple_of(s * 512, 512), 512)],
                    WB[s, pl.ds(0, 512), cols], preferred_element_type=F32,
                )

            PS[g, :, cols] = lax.fori_loop(0, 8, body, jnp.zeros((256, 256), F32)).astype(BF16)

    back = [remote(PS.at[g], PR.at[g], yp_s.at[g], yp_r.at[g], partner) for g in range(2)]

    def take_relay(q):
        for cp in groups[q]:
            cp.wait_recv()
        relays[q].start()
        if q + 2 < 4:
            for cp in groups[q + 2]:
                cp.start()

    for i in range(N_RING):
        for way in range(2):
            ring[way][i].wait_recv()
            if i + 2 < N_RING:
                if i == 2 and way == 0:
                    cross.wait_recv()
                ring[way][i + 2].start()
        if i == 2:
            l_h.wait()
            h_sib.wait_recv()
            take_relay(0)
            for half in range(2):
                mm_chunk("B", half, z)
                mm_chunk("A", half, z)
            for k in range(3):
                mm_arrival(k)
            for cp in scatter:
                cp.wait_recv()
            for k in range(5):
                rows = pl.ds(k * 16, 16)
                own = dec[pl.ds(pl.multiple_of(x * 80 + k * 16, 16), 16), :]
                ysend[rows, :] = (own + rsb[0, rows, :] + rsb[1, rows, :] + rsb[2, rows, :]).astype(BF16)
            ysum.start()
        elif i > 2:
            mm_arrival(i)
        if i == 3:
            mean_squares(0)
        if i == 4:
            mean_squares(1)
        if i == 5:
            ysum.wait_recv()
            for k in range(5):
                rows = pl.ds(k * 16, 16)
                mean[pl.ds(pl.multiple_of(x * 80 + k * 16, 16), 16), :] = (
                    ysend[rows, :].astype(F32) + yrecv[rows, :].astype(F32)
                ) * 0.125
            for cp in spread:
                cp.start()
        if i == 6:
            take_relay(1)
        if i == 8:
            relays[0].wait_recv()
            relays[1].wait_recv()
            partner_sums(0)
            back[0].start()
            take_relay(2)
        if i == 9:
            for cp in spread:
                cp.wait_recv()
            l_m.wait()

            @pl.loop(0, 20)
            def _(k):
                rows = pl.ds(pl.multiple_of(k * 16, 16), 16)
                md = mean[rows, :]
                new_m = 0.9 * mo[rows, :] + md
                nm[rows, :] = new_m
                ng[rows, :] = gl[rows, :] - 0.7 * (0.9 * new_m + md)

            o_m = pltpu.make_async_copy(nm, nm_out, loc.at[5])
            o_g = pltpu.make_async_copy(ng, ng_out, loc.at[6])
            o_m.start()
            o_g.start()
        if i == 11:
            take_relay(3)
            relays[2].wait_recv()
            relays[3].wait_recv()
            partner_sums(1)
            back[1].start()

    def finish(core, g):
        rows = pl.ds(pl.multiple_of(core * 256 + g * 128, 128), 128)
        total = acc[rows, :] + PR[g, pl.ds(pl.multiple_of(core * 128, 128), 128), :].astype(F32)
        return (total * inv[rows, :][:, :1]).astype(BF16)

    swap = [
        remote(
            KS.at[pl.ds(g * 128, 128)], KO.at[pl.ds(g * 128, 128), own_cols], sib_s.at[2 + g], sib_r.at[2 + g], sib
        )
        for g in range(2)
    ]
    for g in range(2):
        back[g].wait_recv()
        KS[pl.ds(g * 128, 128), :] = finish(o, g)
        swap[g].start()
        KO[pl.ds(g * 128, 128), own_cols] = finish(c, g)
    for g in range(2):
        swap[g].wait_recv()
    o_k = pltpu.make_async_copy(KO, keys_out, loc.at[7])
    o_k.start()

    w_sib.wait_send()
    h_sib.wait_send()
    cross.wait_send()
    ysum.wait_send()
    for cp in [cp for grp in groups for cp in grp] + relays + ring[0] + ring[1] + back + scatter + spread + swap:
        cp.wait_send()
    o_m.wait()
    o_g.wait()
    o_k.wait()


def shards(hidden, norm_gain, local_weight, global_weight, momentum):
    weight_rows = local_weight[0]
    own = weight_rows.shape[0]
    gain = lax.dynamic_slice(norm_gain, (lax.axis_index("fsdp") * own,), (own,))
    scaled = (weight_rows.astype(F32) * gain[:, None]).astype(BF16)
    dma = pltpu.SemaphoreType.DMA
    V = pltpu.VMEM
    return tuple(pl.pallas_call(
        kernel,
        out_shape=(
            jax.ShapeDtypeStruct((256, 1024), BF16),
            jax.ShapeDtypeStruct((320, 1024), F32),
            jax.ShapeDtypeStruct((320, 1024), F32),
        ),
        in_specs=[pl.BlockSpec(memory_space=pl.ANY)] * 5,
        out_specs=(pl.BlockSpec(memory_space=pl.ANY),) * 3,
        scratch_shapes=[
            V((512, 10240), BF16), V((2, 256, 4096), BF16), V((8, 640, 512), BF16), V((8, 128, 512), BF16),
            V((512, 512), F32), V((2, 256, 512), BF16), V((2, 256, 512), BF16),
            V((320, 1024), BF16), V((320, 1024), F32), V((320, 1024), F32), V((320, 1024), F32),
            V((3, 80, 1024), F32), V((80, 1024), BF16), V((80, 1024), BF16), V((320, 1024), F32),
            V((320, 1024), F32), V((320, 1024), F32), V((512, 128), F32), V((256, 1024), BF16), V((256, 512), BF16),
            dma((8,)), dma((4,)), dma((4,)), dma((4,)), dma((4,)), dma((2, N_RING)), dma((2, N_RING)),
            dma, dma, dma((4, 4)), dma((4, 4)), dma((2,)), dma((2,)), dma((3,)), dma((3,)), dma((3,)), dma((3,)),
            dma, dma,
        ],
        compiler_params=pltpu.CompilerParams(
            collective_id=0, has_side_effects=True, vmem_limit_bytes=58 * 1024 * 1024
        ),
        cost_estimate=pl.CostEstimate(flops=5368709120, bytes_accessed=12000000, transcendentals=512),
    )(scaled, hidden, weight_rows, global_weight, momentum))


def solution(mesh):
    return jax.shard_map(
        shards,
        mesh=mesh,
        in_specs=(
            P(("replica", "fsdp"), None),
            P(),
            P("replica", "fsdp", None),
            P("fsdp", None),
            P("fsdp", None),
        ),
        out_specs=(P(("replica", "fsdp"), None), P("fsdp", None), P("fsdp", None)),
        check_vma=False,
    )
```

```python
import functools
import math

import jax
import jax.numpy as jnp
from jax import lax
from jax.experimental import pallas as pl
from jax.experimental.pallas import tpu as pltpu
from jax.sharding import PartitionSpec as P

MESH = pl.DeviceIdType.MESH
BLOCK = 128
F32 = jnp.float32
BF16 = jnp.bfloat16

RING = (
    ("B", 0, 0), ("B", 1, 0), ("B", 0, 1), ("B", 1, 1), ("A", 0, 0), ("A", 1, 0), ("B", 0, 2),
    ("B", 1, 2), ("B", 0, 3), ("A", 0, 1), ("A", 1, 1), ("A", 0, 2), ("A", 1, 2), ("A", 0, 3),
)
N_RING = len(RING)
RELAY_AT = (2, 4, 7, 9)
SUM_AT = (8, 9)
HID_FIRST = 3
HID_NEXT = (2, 2, 2, 2, 1, 1, 2, 2, 0, 0, 0, 0, 0, 0)


def kernel(
    gain_in, hid, wl_in, g_in, m_in, keys_out, ng_out, nm_out,
    gain, SX, H, HP, WB, WX, acc, PS, PR, wl, gl, mo, dec, rsb, ysend, yrecv, mean, ng, nm, inv, KO, KS,
    loc, sib_s, sib_r, rel_s, rel_r, z_s, z_r, yc_s, yc_r, yh_s, yh_r, yp_s, yp_r, x_s, x_r, xg_s, xg_r, yl_s, yl_r,
):
    replica, fsdp = lax.axis_index("replica"), lax.axis_index("fsdp")
    x, ylo = lax.rem(replica, 4), lax.div(replica, 4)
    c, z, r = lax.rem(fsdp, 2), lax.rem(lax.div(fsdp, 2), 8), lax.div(fsdp, 16)
    o = 1 - c

    def at_fsdp(r_, z_, c_):
        return (replica, r_ * 16 + z_ * 2 + c_)

    sib = at_fsdp(r, z, o)
    zdev = (at_fsdp(r, lax.rem(z + 1, 8), c), at_fsdp(r, lax.rem(z + 7, 8), c))
    partner = at_fsdp(1 - r, z, c)
    xdev = [(ylo * 4 + lax.rem(x + j, 4), fsdp) for j in (1, 2, 3)]
    ydev = ((1 - ylo) * 4 + x, fsdp)

    def remote(src, dst, s, rcv, dev):
        return pltpu.make_async_remote_copy(
            src_ref=src, dst_ref=dst, send_sem=s, recv_sem=rcv, device_id=dev, device_id_type=MESH
        )

    l_h = pltpu.make_async_copy(hid, H.at[pl.ds(pl.multiple_of(c * 256, 256), 256)], loc.at[0])
    own_cols = pl.ds(pl.multiple_of(c * 512, 512), 512)
    oth_cols = pl.ds(pl.multiple_of(o * 512, 512), 512)
    own_rows = pl.ds(pl.multiple_of(c * 320, 64), 320)
    l_gain = pltpu.make_async_copy(gain_in, gain, loc.at[1])
    l_wl = pltpu.make_async_copy(wl_in, wl, loc.at[2])
    l_g = pltpu.make_async_copy(g_in, gl, loc.at[3])
    l_m = pltpu.make_async_copy(m_in, mo, loc.at[4])
    l_wl.start()
    l_gain.start()

    barrier = pltpu.get_barrier_semaphore()
    everyone = [sib, zdev[0], zdev[1], partner, ydev] + xdev
    for dev in everyone:
        pl.semaphore_signal(barrier, inc=1, device_id=dev, device_id_type=MESH)

    l_wl.wait()
    l_gain.wait()

    @pl.loop(0, 5)
    def _(i):
        rows = pl.ds(pl.multiple_of(i * 64, 64), 64)
        unit = c * 5 + i
        along = gain[pl.ds((r * 8 + z) * 5 + lax.div(unit, 2), 1), :]
        lane = lax.broadcasted_iota(jnp.int32, (64, 128), 1)
        row = lax.broadcasted_iota(jnp.int32, (64, 128), 0)
        mine = lane - row == 64 * lax.rem(unit, 2)
        column = jnp.sum(jnp.where(mine, jnp.broadcast_to(along, (64, 128)), 0.0), axis=-1, keepdims=True)
        SX[rows, :] = (wl[rows, oth_cols].astype(F32) * column).astype(BF16)
        WB[z, pl.ds(pl.multiple_of(c * 320 + i * 64, 64), 64), :] = (wl[rows, own_cols].astype(F32) * column).astype(BF16)

    l_g.start()
    l_h.start()
    l_m.start()
    pl.semaphore_wait(barrier, len(everyone))
    w_sib = remote(SX, WB.at[z, own_rows], sib_s.at[0], sib_r.at[0], sib)
    w_sib.start()
    def hid_group(q):
        g, half = divmod(q, 2)
        out = []
        for zb in range(half * 4, half * 4 + 4):
            col = pl.multiple_of((1 - r) * 5120 + zb * 640, 128)
            out.append(remote(
                hid.at[pl.ds(g * 128, 128), pl.ds(col, 512)],
                HP.at[g, pl.ds(pl.multiple_of(c * 128, 128), 128), pl.ds(zb * 512, 512)],
                yh_s.at[q, zb % 4], yh_r.at[q, zb % 4], partner,
            ))
        return out

    def relay(q):
        g, half = divmod(q, 2)
        part = HP.at[g, pl.ds(pl.multiple_of(c * 128, 128), 128), pl.ds(half * 2048, 2048)]
        return remote(part, part, rel_s.at[q], rel_r.at[q], sib)

    groups = [hid_group(q) for q in range(4)]
    relays = [relay(q) for q in range(4)]
    queue = [cp for grp in groups for cp in grp]

    def send_hidden(count):
        for _ in range(min(count, len(queue))):
            queue.pop(0).start()

    send_hidden(HID_FIRST)


    def chunk_ref(kind, half, slot):
        if kind == "B":
            return WB.at[slot, pl.ds(half * 256, 256)]
        if half == 0:
            return WB.at[slot, pl.ds(512, 128)]
        return WX.at[slot]

    def slot_of(way, dist):
        return lax.rem(z + (8 - dist if way == 0 else dist), 8)

    def ring_copy(way, i):
        kind, half, dist = RING[i]
        part = chunk_ref(kind, half if way == 0 else 1 - half, slot_of(way, dist))
        return remote(part, part, z_s.at[way, i], z_r.at[way, i], zdev[way])

    ring = [[ring_copy(way, i) for i in range(N_RING)] for way in range(2)]

    w_sib.wait_recv()
    for i in range(2):
        for way in range(2):
            ring[way][i].start()
    cross = remote(WB.at[z, pl.ds(512, 128)], WX.at[z], yc_s, yc_r, partner)
    cross.start()
    h_sib = remote(
        hid, H.at[pl.ds(pl.multiple_of(c * 256, 256), 256)], sib_s.at[1], sib_r.at[1], sib
    )
    h_sib.start()

    l_g.wait()

    @pl.loop(0, 20)
    def _(i):
        rows = pl.ds(pl.multiple_of(i * 16, 16), 16)
        for b in range(8):
            cols = pl.ds(b * BLOCK, BLOCK)
            d = gl[rows, cols] - wl[rows, cols].astype(F32)
            s = (jnp.max(jnp.abs(d), axis=-1, keepdims=True) + 1e-06).astype(BF16).astype(F32)
            dec[rows, cols] = (d / s).astype(BF16).astype(F32) * s

    def quarter(q):
        return pl.ds(pl.multiple_of(q * 80, 16), 80)

    scatter = [
        remote(dec.at[quarter(lax.rem(x + j, 4))], rsb.at[j - 1], x_s.at[j - 1], x_r.at[j - 1], xdev[j - 1])
        for j in (1, 2, 3)
    ]
    for cp in scatter:
        cp.start()
    ysum = remote(ysend, yrecv, yl_s, yl_r, ydev)
    spread = [
        remote(mean.at[quarter(x)], mean.at[quarter(x)], xg_s.at[j - 1], xg_r.at[j - 1], xdev[j - 1])
        for j in (1, 2, 3)
    ]
    acc[...] = jnp.zeros_like(acc)

    def mm(h_col, w_ref, depth):
        for n in range(2):
            cols = pl.ds(n * 256, 256)
            acc[:, cols] += jnp.dot(
                H[:, pl.ds(pl.multiple_of(h_col, 128), depth)], w_ref[:, cols], preferred_element_type=F32
            )

    def mm_chunk(kind, half, slot):
        base = slot * 640
        if kind == "B":
            mm(r * 5120 + base + half * 256, chunk_ref(kind, half, slot), 256)
        elif half == 0:
            mm(r * 5120 + base + 512, chunk_ref(kind, half, slot), 128)
        else:
            mm((1 - r) * 5120 + base + 512, chunk_ref(kind, half, slot), 128)

    def mm_arrival(i):
        kind, half, dist = RING[i]
        if kind == "B":
            @pl.loop(0, 2)
            def _(way):
                slot = lax.rem(z + 8 + (2 * way - 1) * (dist + 1), 8)
                h_ = way if half == 0 else 1 - way
                mm(
                    r * 5120 + slot * 640 + h_ * 256,
                    WB.at[slot, pl.ds(pl.multiple_of(h_ * 256, 256), 256)], 256,
                )
        else:
            for way in range(2):
                mm_chunk(kind, half if way == 0 else 1 - half, slot_of(way, dist + 1))

    def mean_squares(part):
        @pl.loop(0, 4)
        def _(k):
            rows = pl.ds(pl.multiple_of(part * 256 + k * 64, 64), 64)

            def body(k, total):
                for s in range(4):
                    v = H[rows, pl.ds(pl.multiple_of(k * 512 + s * 128, 128), 128)].astype(F32)
                    total = total + v * v
                return total

            total = lax.fori_loop(0, 20, body, jnp.zeros((64, 128), F32))
            ms = jnp.sum(total, axis=-1, keepdims=True) * (1.0 / 10240)
            inv[rows, :] = jnp.broadcast_to(lax.rsqrt(ms + 1e-05) * (1.0 / math.sqrt(10240)), (64, 128))

    def partner_sums(g):
        for n in range(2):
            cols = pl.ds(n * 256, 256)

            def body(s, total):
                return total + jnp.dot(
                    HP[g, :, pl.ds(pl.multiple_of(s * 512, 512), 512)],
                    WB[s, pl.ds(0, 512), cols], preferred_element_type=F32,
                )

            PS[g, :, cols] = lax.fori_loop(0, 8, body, jnp.zeros((256, 256), F32)).astype(BF16)

    back = [remote(PS.at[g], PR.at[g], yp_s.at[g], yp_r.at[g], partner) for g in range(2)]

    def take_relay(q):
        for cp in groups[q]:
            cp.wait_recv()
        relays[q].start()

    for i in range(N_RING):
        for way in range(2):
            ring[way][i].wait_recv()
            if i + 2 < N_RING:
                if i == 2 and way == 0:
                    cross.wait_recv()
                ring[way][i + 2].start()
        send_hidden(HID_NEXT[i])
        for q in range(4):
            if RELAY_AT[q] == i:
                take_relay(q)
        if i == 2:
            h_sib.wait_recv()
            for half in range(2):
                mm_chunk("B", half, z)
                mm_chunk("A", half, z)
            for k in range(3):
                mm_arrival(k)
            for cp in scatter:
                cp.wait_recv()
            for k in range(5):
                rows = pl.ds(k * 16, 16)
                own = dec[pl.ds(pl.multiple_of(x * 80 + k * 16, 16), 16), :]
                ysend[rows, :] = (own + rsb[0, rows, :] + rsb[1, rows, :] + rsb[2, rows, :]).astype(BF16)
            ysum.start()
        elif i > 2:
            mm_arrival(i)
        if i == 0:
            l_h.wait()
            mean_squares(c)
        if i == 3:
            mean_squares(o)
        if i == 5:
            ysum.wait_recv()
            for k in range(5):
                rows = pl.ds(k * 16, 16)
                mean[pl.ds(pl.multiple_of(x * 80 + k * 16, 16), 16), :] = (
                    ysend[rows, :].astype(F32) + yrecv[rows, :].astype(F32)
                ) * 0.125
            for cp in spread:
                cp.start()
        if i == SUM_AT[0]:
            relays[0].wait_recv()
            relays[1].wait_recv()
            partner_sums(0)
            back[0].start()
        if i == 9:
            for cp in spread:
                cp.wait_recv()
            l_m.wait()

            @pl.loop(0, 20)
            def _(k):
                rows = pl.ds(pl.multiple_of(k * 16, 16), 16)
                md = mean[rows, :]
                new_m = 0.9 * mo[rows, :] + md
                nm[rows, :] = new_m
                ng[rows, :] = gl[rows, :] - 0.7 * (0.9 * new_m + md)

            o_m = pltpu.make_async_copy(nm, nm_out, loc.at[5])
            o_g = pltpu.make_async_copy(ng, ng_out, loc.at[6])
            o_m.start()
            o_g.start()
        if i == SUM_AT[1]:
            relays[2].wait_recv()
            relays[3].wait_recv()
            partner_sums(1)
            back[1].start()

    def finish(core, g):
        rows = pl.ds(pl.multiple_of(core * 256 + g * 128, 128), 128)
        total = acc[rows, :] + PR[g, pl.ds(pl.multiple_of(core * 128, 128), 128), :].astype(F32)
        return (total * inv[rows, :][:, :1]).astype(BF16)

    swap = [
        remote(
            KS.at[pl.ds(g * 128, 128)], KO.at[pl.ds(g * 128, 128), own_cols], sib_s.at[2 + g], sib_r.at[2 + g], sib
        )
        for g in range(2)
    ]
    for g in range(2):
        back[g].wait_recv()
        KS[pl.ds(g * 128, 128), :] = finish(o, g)
        swap[g].start()
        KO[pl.ds(g * 128, 128), own_cols] = finish(c, g)
    for g in range(2):
        swap[g].wait_recv()
    o_k = pltpu.make_async_copy(KO, keys_out, loc.at[7])
    o_k.start()

    w_sib.wait_send()
    h_sib.wait_send()
    cross.wait_send()
    ysum.wait_send()
    for cp in [cp for grp in groups for cp in grp] + relays + ring[0] + ring[1] + back + scatter + spread + swap:
        cp.wait_send()
    o_m.wait()
    o_g.wait()
    o_k.wait()


def shards(hidden, norm_gain, local_weight, global_weight, momentum):
    weight_rows = local_weight[0]
    dma = pltpu.SemaphoreType.DMA
    V = pltpu.VMEM
    return tuple(pl.pallas_call(
        kernel,
        out_shape=(
            jax.ShapeDtypeStruct((256, 1024), BF16),
            jax.ShapeDtypeStruct((320, 1024), F32),
            jax.ShapeDtypeStruct((320, 1024), F32),
        ),
        in_specs=[pl.BlockSpec(memory_space=pl.ANY)] * 5,
        out_specs=(pl.BlockSpec(memory_space=pl.ANY),) * 3,
        scratch_shapes=[
            V((80, 128), F32), V((320, 512), BF16), V((512, 10240), BF16), V((2, 256, 4096), BF16), V((8, 640, 512), BF16), V((8, 128, 512), BF16),
            V((512, 512), F32), V((2, 256, 512), BF16), V((2, 256, 512), BF16),
            V((320, 1024), BF16), V((320, 1024), F32), V((320, 1024), F32), V((320, 1024), F32),
            V((3, 80, 1024), F32), V((80, 1024), BF16), V((80, 1024), BF16), V((320, 1024), F32),
            V((320, 1024), F32), V((320, 1024), F32), V((512, 128), F32), V((256, 1024), BF16), V((256, 512), BF16),
            dma((8,)), dma((4,)), dma((4,)), dma((4,)), dma((4,)), dma((2, N_RING)), dma((2, N_RING)),
            dma, dma, dma((4, 4)), dma((4, 4)), dma((2,)), dma((2,)), dma((3,)), dma((3,)), dma((3,)), dma((3,)),
            dma, dma,
        ],
        compiler_params=pltpu.CompilerParams(
            collective_id=0, has_side_effects=True, vmem_limit_bytes=50 * 1024 * 1024
        ),
        cost_estimate=pl.CostEstimate(flops=5368709120, bytes_accessed=12000000, transcendentals=512),
    )(norm_gain.reshape(80, 128), hidden, weight_rows, global_weight, momentum))


def solution(mesh):
    return jax.shard_map(
        shards,
        mesh=mesh,
        in_specs=(
            P(("replica", "fsdp"), None),
            P(),
            P("replica", "fsdp", None),
            P("fsdp", None),
            P("fsdp", None),
        ),
        out_specs=(P(("replica", "fsdp"), None), P("fsdp", None), P("fsdp", None)),
        check_vma=False,
    )
```

```python
import functools
import math

import jax
import jax.numpy as jnp
from jax import lax
from jax.experimental import pallas as pl
from jax.experimental.pallas import tpu as pltpu
from jax.sharding import PartitionSpec as P

MESH = pl.DeviceIdType.MESH
BLOCK = 128
F32 = jnp.float32
BF16 = jnp.bfloat16

RING = (
    ("B", 0, 0), ("B", 1, 0), ("B", 0, 1), ("B", 1, 1), ("A", 0, 0), ("A", 1, 0), ("B", 0, 2),
    ("B", 1, 2), ("B", 0, 3), ("A", 0, 1), ("A", 1, 1), ("A", 0, 2), ("A", 1, 2), ("A", 0, 3),
)
N_RING = len(RING)
RELAY_AT = (2, 4, 7, 10)
SUM_AT = (8, 10)
STATE_AT = 11
HID_FIRST = 3
HID_NEXT = (2, 2, 2, 2, 1, 1, 2, 2, 0, 0, 0, 0, 0, 0)


def kernel(
    gain_in, hid, wl_in, g_in, m_in, keys_out, ng_out, nm_out,
    gain, SX, H, HP, WB, WX, acc, accp, PS, PR, wl, gl, mo, dec, rsb, ysend, yrecv, mean, ng, nm, inv, KO, KS,
    loc, sib_s, sib_r, rel_s, rel_r, z_s, z_r, yc_s, yc_r, yh_s, yh_r, yp_s, yp_r, x_s, x_r, xg_s, xg_r, yl_s, yl_r,
):
    replica, fsdp = lax.axis_index("replica"), lax.axis_index("fsdp")
    x, ylo = lax.rem(replica, 4), lax.div(replica, 4)
    c, z, r = lax.rem(fsdp, 2), lax.rem(lax.div(fsdp, 2), 8), lax.div(fsdp, 16)
    o = 1 - c

    def at_fsdp(r_, z_, c_):
        return (replica, r_ * 16 + z_ * 2 + c_)

    sib = at_fsdp(r, z, o)
    zdev = (at_fsdp(r, lax.rem(z + 1, 8), c), at_fsdp(r, lax.rem(z + 7, 8), c))
    partner = at_fsdp(1 - r, z, c)
    xdev = [(ylo * 4 + lax.rem(x + j, 4), fsdp) for j in (1, 2, 3)]
    ydev = ((1 - ylo) * 4 + x, fsdp)

    def remote(src, dst, s, rcv, dev):
        return pltpu.make_async_remote_copy(
            src_ref=src, dst_ref=dst, send_sem=s, recv_sem=rcv, device_id=dev, device_id_type=MESH
        )

    l_h = pltpu.make_async_copy(hid, H.at[pl.ds(pl.multiple_of(c * 256, 256), 256)], loc.at[0])
    own_cols = pl.ds(pl.multiple_of(c * 512, 512), 512)
    oth_cols = pl.ds(pl.multiple_of(o * 512, 512), 512)
    own_rows = pl.ds(pl.multiple_of(c * 320, 64), 320)
    l_gain = pltpu.make_async_copy(gain_in, gain, loc.at[1])
    l_wl = pltpu.make_async_copy(wl_in, wl, loc.at[2])
    l_g = pltpu.make_async_copy(g_in, gl, loc.at[3])
    l_m = pltpu.make_async_copy(m_in, mo, loc.at[4])
    l_wl.start()
    l_gain.start()

    barrier = pltpu.get_barrier_semaphore()
    everyone = [sib, zdev[0], zdev[1], partner, ydev] + xdev
    for dev in everyone:
        pl.semaphore_signal(barrier, inc=1, device_id=dev, device_id_type=MESH)

    l_wl.wait()
    l_gain.wait()

    @pl.loop(0, 5)
    def _(i):
        rows = pl.ds(pl.multiple_of(i * 64, 64), 64)
        unit = c * 5 + i
        along = gain[pl.ds((r * 8 + z) * 5 + lax.div(unit, 2), 1), :]
        lane = lax.broadcasted_iota(jnp.int32, (64, 128), 1)
        row = lax.broadcasted_iota(jnp.int32, (64, 128), 0)
        mine = lane - row == 64 * lax.rem(unit, 2)
        column = jnp.sum(jnp.where(mine, jnp.broadcast_to(along, (64, 128)), 0.0), axis=-1, keepdims=True)
        SX[rows, :] = (wl[rows, oth_cols].astype(F32) * column).astype(BF16)
        WB[z, pl.ds(pl.multiple_of(c * 320 + i * 64, 64), 64), :] = (wl[rows, own_cols].astype(F32) * column).astype(BF16)

    l_g.start()
    l_h.start()
    l_m.start()
    pl.semaphore_wait(barrier, len(everyone))
    w_sib = remote(SX, WB.at[z, own_rows], sib_s.at[0], sib_r.at[0], sib)
    w_sib.start()
    def hid_group(q):
        g, half = divmod(q, 2)
        out = []
        for zb in range(half * 4, half * 4 + 4):
            col = pl.multiple_of((1 - r) * 5120 + zb * 640, 128)
            out.append(remote(
                hid.at[pl.ds(g * 128, 128), pl.ds(col, 512)],
                HP.at[g, pl.ds(pl.multiple_of(c * 128, 128), 128), pl.ds(zb * 512, 512)],
                yh_s.at[q, zb % 4], yh_r.at[q, zb % 4], partner,
            ))
        return out

    def relay(q):
        g, half = divmod(q, 2)
        part = HP.at[g, pl.ds(pl.multiple_of(c * 128, 128), 128), pl.ds(half * 2048, 2048)]
        return remote(part, part, rel_s.at[q], rel_r.at[q], sib)

    groups = [hid_group(q) for q in range(4)]
    relays = [relay(q) for q in range(4)]
    queue = [cp for grp in groups for cp in grp]

    def send_hidden(count):
        for _ in range(min(count, len(queue))):
            queue.pop(0).start()

    send_hidden(HID_FIRST)


    def chunk_ref(kind, half, slot):
        if kind == "B":
            return WB.at[slot, pl.ds(half * 256, 256)]
        if half == 0:
            return WB.at[slot, pl.ds(512, 128)]
        return WX.at[slot]

    def slot_of(way, dist):
        return lax.rem(z + (8 - dist if way == 0 else dist), 8)

    def ring_copy(way, i):
        kind, half, dist = RING[i]
        part = chunk_ref(kind, half if way == 0 else 1 - half, slot_of(way, dist))
        return remote(part, part, z_s.at[way, i], z_r.at[way, i], zdev[way])

    ring = [[ring_copy(way, i) for i in range(N_RING)] for way in range(2)]

    w_sib.wait_recv()
    for i in range(2):
        for way in range(2):
            ring[way][i].start()
    cross = remote(WB.at[z, pl.ds(512, 128)], WX.at[z], yc_s, yc_r, partner)
    cross.start()
    h_sib = remote(
        hid, H.at[pl.ds(pl.multiple_of(c * 256, 256), 256)], sib_s.at[1], sib_r.at[1], sib
    )
    h_sib.start()

    l_g.wait()

    @pl.loop(0, 20)
    def _(i):
        rows = pl.ds(pl.multiple_of(i * 16, 16), 16)
        for b in range(8):
            cols = pl.ds(b * BLOCK, BLOCK)
            d = gl[rows, cols] - wl[rows, cols].astype(F32)
            s = (jnp.max(jnp.abs(d), axis=-1, keepdims=True) + 1e-06).astype(BF16).astype(F32)
            dec[rows, cols] = (d / s).astype(BF16).astype(F32) * s

    def quarter(q):
        return pl.ds(pl.multiple_of(q * 80, 16), 80)

    scatter = [
        remote(dec.at[quarter(lax.rem(x + j, 4))], rsb.at[j - 1], x_s.at[j - 1], x_r.at[j - 1], xdev[j - 1])
        for j in (1, 2, 3)
    ]
    for cp in scatter:
        cp.start()
    ysum = remote(ysend, yrecv, yl_s, yl_r, ydev)
    spread = [
        remote(mean.at[quarter(x)], mean.at[quarter(x)], xg_s.at[j - 1], xg_r.at[j - 1], xdev[j - 1])
        for j in (1, 2, 3)
    ]
    acc[...] = jnp.zeros_like(acc)

    def mm(h_col, w_ref, depth):
        for n in range(2):
            cols = pl.ds(n * 256, 256)
            acc[:, cols] += jnp.dot(
                H[:, pl.ds(pl.multiple_of(h_col, 128), depth)], w_ref[:, cols], preferred_element_type=F32
            )

    def mm_chunk(kind, half, slot):
        base = slot * 640
        if kind == "B":
            mm(r * 5120 + base + half * 256, chunk_ref(kind, half, slot), 256)
        elif half == 0:
            mm(r * 5120 + base + 512, chunk_ref(kind, half, slot), 128)
        else:
            mm((1 - r) * 5120 + base + 512, chunk_ref(kind, half, slot), 128)

    def mm_arrival(i):
        kind, half, dist = RING[i]
        if kind == "B":
            @pl.loop(0, 2)
            def _(way):
                slot = lax.rem(z + 8 + (2 * way - 1) * (dist + 1), 8)
                h_ = way if half == 0 else 1 - way
                mm(
                    r * 5120 + slot * 640 + h_ * 256,
                    WB.at[slot, pl.ds(pl.multiple_of(h_ * 256, 256), 256)], 256,
                )
        else:
            for way in range(2):
                mm_chunk(kind, half if way == 0 else 1 - half, slot_of(way, dist + 1))

    def mean_squares(part):
        @pl.loop(0, 4)
        def _(k):
            rows = pl.ds(pl.multiple_of(part * 256 + k * 64, 64), 64)

            def body(k, total):
                for s in range(4):
                    v = H[rows, pl.ds(pl.multiple_of(k * 512 + s * 128, 128), 128)].astype(F32)
                    total = total + v * v
                return total

            total = lax.fori_loop(0, 20, body, jnp.zeros((64, 128), F32))
            ms = jnp.sum(total, axis=-1, keepdims=True) * (1.0 / 10240)
            inv[rows, :] = jnp.broadcast_to(lax.rsqrt(ms + 1e-05) * (1.0 / math.sqrt(10240)), (64, 128))

    def partner_mm(g, slot, first=False):
        left = HP[g, :, pl.ds(pl.multiple_of(slot * 512, 512), 512)]
        for n in range(2):
            cols = pl.ds(n * 256, 256)
            part = jnp.dot(left, WB[slot, pl.ds(0, 512), cols], preferred_element_type=F32)
            accp[:, cols] = part if first else accp[:, cols] + part

    back = [
        [
            remote(
                PS.at[g, pl.ds(pl.multiple_of(core * 128, 128), 128)],
                PR.at[g, pl.ds(pl.multiple_of(core * 128, 128), 128)],
                yp_s.at[g, k], yp_r.at[g, k], partner,
            )
            for k, core in enumerate((o, c))
        ]
        for g in range(2)
    ]

    def send_back(g):
        PS[g] = accp[...].astype(BF16)
        for cp in back[g]:
            cp.start()


    def take_relay(q):
        for cp in groups[q]:
            cp.wait_recv()
        relays[q].start()

    for i in range(N_RING):
        for way in range(2):
            ring[way][i].wait_recv()
            if i + 2 < N_RING:
                if i == 2 and way == 0:
                    cross.wait_recv()
                ring[way][i + 2].start()
        send_hidden(HID_NEXT[i])
        for q in range(4):
            if RELAY_AT[q] == i:
                take_relay(q)
        if i == 2:
            h_sib.wait_recv()
            for half in range(2):
                mm_chunk("B", half, z)
                mm_chunk("A", half, z)
            for k in range(3):
                mm_arrival(k)
            for cp in scatter:
                cp.wait_recv()
            for k in range(5):
                rows = pl.ds(k * 16, 16)
                own = dec[pl.ds(pl.multiple_of(x * 80 + k * 16, 16), 16), :]
                ysend[rows, :] = (own + rsb[0, rows, :] + rsb[1, rows, :] + rsb[2, rows, :]).astype(BF16)
            ysum.start()
        elif i > 2:
            mm_arrival(i)
        if i == 0:
            l_h.wait()
            mean_squares(c)
        if i == 3:
            mean_squares(o)
        if i == 5:
            ysum.wait_recv()
            for k in range(5):
                rows = pl.ds(k * 16, 16)
                mean[pl.ds(pl.multiple_of(x * 80 + k * 16, 16), 16), :] = (
                    ysend[rows, :].astype(F32) + yrecv[rows, :].astype(F32)
                ) * 0.125
            for cp in spread:
                cp.start()
        if i == SUM_AT[0] - 2:
            relays[0].wait_recv()
            relays[1].wait_recv()
            partner_mm(0, z, first=True)

            @pl.loop(0, 4)
            def _(k):
                partner_mm(0, lax.rem(z + jnp.where(k < 2, k + 1, k + 4), 8))

        if i == SUM_AT[0] - 1:
            @pl.loop(0, 2)
            def _(k):
                partner_mm(0, lax.rem(z + 3 + 2 * k, 8))

        if i == SUM_AT[0]:
            partner_mm(0, lax.rem(z + 4, 8))
            send_back(0)
            relays[2].wait_recv()
            partner_mm(1, 0, first=True)

            @pl.loop(1, 4)
            def _(k):
                partner_mm(1, k)

        if i == STATE_AT:
            for cp in spread:
                cp.wait_recv()
            l_m.wait()

            @pl.loop(0, 20)
            def _(k):
                rows = pl.ds(pl.multiple_of(k * 16, 16), 16)
                md = mean[rows, :]
                new_m = 0.9 * mo[rows, :] + md
                nm[rows, :] = new_m
                ng[rows, :] = gl[rows, :] - 0.7 * (0.9 * new_m + md)

            o_m = pltpu.make_async_copy(nm, nm_out, loc.at[5])
            o_g = pltpu.make_async_copy(ng, ng_out, loc.at[6])
            o_m.start()
            o_g.start()
        if i == SUM_AT[1]:
            relays[3].wait_recv()

            @pl.loop(4, 8)
            def _(k):
                partner_mm(1, k)

            send_back(1)

    def finish(core, g):
        rows = pl.ds(pl.multiple_of(core * 256 + g * 128, 128), 128)
        total = acc[rows, :] + PR[g, pl.ds(pl.multiple_of(core * 128, 128), 128), :].astype(F32)
        return (total * inv[rows, :][:, :1]).astype(BF16)

    swap = [
        remote(
            KS.at[pl.ds(g * 128, 128)], KO.at[pl.ds(g * 128, 128), own_cols], sib_s.at[2 + g], sib_r.at[2 + g], sib
        )
        for g in range(2)
    ]
    for g in range(2):
        back[g][0].wait_recv()
        KS[pl.ds(g * 128, 128), :] = finish(o, g)
        swap[g].start()
        back[g][1].wait_recv()
        KO[pl.ds(g * 128, 128), own_cols] = finish(c, g)
    for g in range(2):
        swap[g].wait_recv()
    o_k = pltpu.make_async_copy(KO, keys_out, loc.at[7])
    o_k.start()

    w_sib.wait_send()
    h_sib.wait_send()
    cross.wait_send()
    ysum.wait_send()
    for cp in [cp for grp in groups for cp in grp] + relays + ring[0] + ring[1] + back[0] + back[1] + scatter + spread + swap:
        cp.wait_send()
    o_m.wait()
    o_g.wait()
    o_k.wait()


def write_out(a, b, c, a_out, b_out, c_out, sems):
    copies = [
        pltpu.make_async_copy(src, dst, sems.at[i])
        for i, (src, dst) in enumerate(((a, a_out), (b, b_out), (c, c_out)))
    ]
    for cp in copies:
        cp.start()
    for cp in copies:
        cp.wait()


def shards(hidden, norm_gain, local_weight, global_weight, momentum):
    weight_rows = local_weight[0]
    dma = pltpu.SemaphoreType.DMA
    V = pltpu.VMEM
    parts = tuple(pl.pallas_call(
        kernel,
        out_shape=(
            jax.ShapeDtypeStruct((256, 1024), BF16),
            jax.ShapeDtypeStruct((320, 1024), F32),
            jax.ShapeDtypeStruct((320, 1024), F32),
        ),
        in_specs=[pl.BlockSpec(memory_space=pl.ANY)] * 5,
        out_specs=(pl.BlockSpec(memory_space=pl.ANY),) * 3,
        scratch_shapes=[
            V((80, 128), F32), V((320, 512), BF16), V((512, 10240), BF16), V((2, 256, 4096), BF16), V((8, 640, 512), BF16), V((8, 128, 512), BF16),
            V((512, 512), F32), V((256, 512), F32), V((2, 256, 512), BF16), V((2, 256, 512), BF16),
            V((320, 1024), BF16), V((320, 1024), F32), V((320, 1024), F32), V((320, 1024), F32),
            V((3, 80, 1024), F32), V((80, 1024), BF16), V((80, 1024), BF16), V((320, 1024), F32),
            V((320, 1024), F32), V((320, 1024), F32), V((512, 128), F32), V((256, 1024), BF16), V((256, 512), BF16),
            dma((8,)), dma((4,)), dma((4,)), dma((4,)), dma((4,)), dma((2, N_RING)), dma((2, N_RING)),
            dma, dma, dma((4, 4)), dma((4, 4)), dma((2, 2)), dma((2, 2)), dma((3,)), dma((3,)), dma((3,)), dma((3,)),
            dma, dma,
        ],
        compiler_params=pltpu.CompilerParams(
            collective_id=0, has_side_effects=True, vmem_limit_bytes=50 * 1024 * 1024
        ),
        cost_estimate=pl.CostEstimate(flops=5368709120, bytes_accessed=12000000, transcendentals=512),
    )(pltpu.with_memory_space_constraint(norm_gain.reshape(80, 128), pltpu.HBM), hidden, pltpu.with_memory_space_constraint(weight_rows, pltpu.HBM), global_weight, momentum))
    return tuple(pl.pallas_call(
        write_out,
        out_shape=tuple(jax.ShapeDtypeStruct(part.shape, part.dtype) for part in parts),
        in_specs=[pl.BlockSpec(memory_space=pltpu.VMEM)] * 3,
        out_specs=(pl.BlockSpec(memory_space=pl.ANY),) * 3,
        scratch_shapes=[dma((3,))],
        compiler_params=pltpu.CompilerParams(vmem_limit_bytes=8 * 1024 * 1024),
    )(*parts))


def solution(mesh):
    return jax.shard_map(
        shards,
        mesh=mesh,
        in_specs=(
            P(("replica", "fsdp"), None),
            P(),
            P("replica", "fsdp", None),
            P("fsdp", None),
            P("fsdp", None),
        ),
        out_specs=(P(("replica", "fsdp"), None), P("fsdp", None), P("fsdp", None)),
        check_vma=False,
    )
```

```python
import functools
import math

import jax
import jax.numpy as jnp
from jax import lax
from jax.experimental import pallas as pl
from jax.experimental.pallas import tpu as pltpu
from jax.sharding import PartitionSpec as P

MESH = pl.DeviceIdType.MESH
BLOCK = 128
F32 = jnp.float32
BF16 = jnp.bfloat16

RING = (
    ("B", 0, 0), ("B", 1, 0), ("B", 0, 1), ("B", 1, 1), ("A", 0, 0), ("A", 1, 0), ("B", 0, 2),
    ("B", 1, 2), ("B", 0, 3), ("A", 0, 1), ("A", 1, 1), ("A", 0, 2), ("A", 1, 2), ("A", 0, 3),
)
N_RING = len(RING)
RELAY_AT = (2, 4, 7, 10)
SUM_AT = (8, 10)
STATE_AT = 11
HID_FIRST = 3
HID_NEXT = (2, 2, 2, 2, 1, 1, 2, 2, 0, 0, 0, 0, 0, 0)


def kernel(
    gain_in, hid, wl_in, g_in, m_in, keys_out, ng_out, nm_out,
    gain, SX, H, HP, WB, WX, acc, accp, PS, PR, wl, gl, mo, dec, rsb, ysend, yrecv, mean, ng, nm, inv, KO, KS,
    loc, hs_s, hs_r, sib_s, sib_r, rel_s, rel_r, z_s, z_r, yc_s, yc_r, yh_s, yh_r, yp_s, yp_r, x_s, x_r, xg_s, xg_r, yl_s, yl_r,
):
    replica, fsdp = lax.axis_index("replica"), lax.axis_index("fsdp")
    x, ylo = lax.rem(replica, 4), lax.div(replica, 4)
    c, z, r = lax.rem(fsdp, 2), lax.rem(lax.div(fsdp, 2), 8), lax.div(fsdp, 16)
    o = 1 - c

    def at_fsdp(r_, z_, c_):
        return (replica, r_ * 16 + z_ * 2 + c_)

    sib = at_fsdp(r, z, o)
    zdev = (at_fsdp(r, lax.rem(z + 1, 8), c), at_fsdp(r, lax.rem(z + 7, 8), c))
    partner = at_fsdp(1 - r, z, c)
    xdev = [(ylo * 4 + lax.rem(x + j, 4), fsdp) for j in (1, 2, 3)]
    ydev = ((1 - ylo) * 4 + x, fsdp)

    def remote(src, dst, s, rcv, dev):
        return pltpu.make_async_remote_copy(
            src_ref=src, dst_ref=dst, send_sem=s, recv_sem=rcv, device_id=dev, device_id_type=MESH
        )

    l_h = pltpu.make_async_copy(hid, H.at[pl.ds(pl.multiple_of(c * 256, 256), 256)], loc.at[0])
    own_cols = pl.ds(pl.multiple_of(c * 512, 512), 512)
    oth_cols = pl.ds(pl.multiple_of(o * 512, 512), 512)
    own_rows = pl.ds(pl.multiple_of(c * 320, 64), 320)
    l_gain = pltpu.make_async_copy(gain_in, gain, loc.at[1])
    l_wl = pltpu.make_async_copy(wl_in, wl, loc.at[2])
    l_g = pltpu.make_async_copy(g_in, gl, loc.at[3])
    l_m = pltpu.make_async_copy(m_in, mo, loc.at[4])
    l_wl.start()
    l_gain.start()

    barrier = pltpu.get_barrier_semaphore()
    everyone = [sib, zdev[0], zdev[1], partner, ydev] + xdev
    for dev in everyone:
        pl.semaphore_signal(barrier, inc=1, device_id=dev, device_id_type=MESH)

    l_wl.wait()
    l_gain.wait()

    @pl.loop(0, 5)
    def _(i):
        rows = pl.ds(pl.multiple_of(i * 64, 64), 64)
        unit = c * 5 + i
        along = gain[pl.ds((r * 8 + z) * 5 + lax.div(unit, 2), 1), :]
        lane = lax.broadcasted_iota(jnp.int32, (64, 128), 1)
        row = lax.broadcasted_iota(jnp.int32, (64, 128), 0)
        mine = lane - row == 64 * lax.rem(unit, 2)
        column = jnp.sum(jnp.where(mine, jnp.broadcast_to(along, (64, 128)), 0.0), axis=-1, keepdims=True)
        SX[rows, :] = (wl[rows, oth_cols].astype(F32) * column).astype(BF16)
        WB[z, pl.ds(pl.multiple_of(c * 320 + i * 64, 64), 64), :] = (wl[rows, own_cols].astype(F32) * column).astype(BF16)

    l_g.start()
    l_h.start()
    l_m.start()
    pl.semaphore_wait(barrier, len(everyone))
    w_sib = remote(SX, WB.at[z, own_rows], sib_s.at[0], sib_r.at[0], sib)
    w_sib.start()
    def hid_group(q):
        g, half = divmod(q, 2)
        out = []
        for zb in range(half * 4, half * 4 + 4):
            col = pl.multiple_of((1 - r) * 5120 + zb * 640, 128)
            out.append(remote(
                hid.at[pl.ds(g * 128, 128), pl.ds(col, 512)],
                HP.at[g, pl.ds(pl.multiple_of(c * 128, 128), 128), pl.ds(zb * 512, 512)],
                yh_s.at[q, zb % 4], yh_r.at[q, zb % 4], partner,
            ))
        return out

    def relay(q):
        g, half = divmod(q, 2)
        part = HP.at[g, pl.ds(pl.multiple_of(c * 128, 128), 128), pl.ds(half * 2048, 2048)]
        return remote(part, part, rel_s.at[q], rel_r.at[q], sib)

    groups = [hid_group(q) for q in range(4)]
    relays = [relay(q) for q in range(4)]
    queue = [cp for grp in groups for cp in grp]

    def send_hidden(count):
        for _ in range(min(count, len(queue))):
            queue.pop(0).start()

    send_hidden(HID_FIRST)


    def chunk_ref(kind, half, slot):
        if kind == "B":
            return WB.at[slot, pl.ds(half * 256, 256)]
        if half == 0:
            return WB.at[slot, pl.ds(512, 128)]
        return WX.at[slot]

    def slot_of(way, dist):
        return lax.rem(z + (8 - dist if way == 0 else dist), 8)

    def ring_copy(way, i):
        kind, half, dist = RING[i]
        part = chunk_ref(kind, half if way == 0 else 1 - half, slot_of(way, dist))
        return remote(part, part, z_s.at[way, i], z_r.at[way, i], zdev[way])

    ring = [[ring_copy(way, i) for i in range(N_RING)] for way in range(2)]

    w_sib.wait_recv()
    for i in range(2):
        for way in range(2):
            ring[way][i].start()
    cross = remote(WB.at[z, pl.ds(512, 128)], WX.at[z], yc_s, yc_r, partner)
    cross.start()
    h_sib = [
        remote(
            hid.at[pl.ds(k * 64, 64)], H.at[pl.ds(pl.multiple_of(c * 256 + k * 64, 64), 64)],
            hs_s.at[k], hs_r.at[k], sib,
        )
        for k in range(4)
    ]
    h_sib[0].start()
    h_sib[1].start()

    l_g.wait()

    @pl.loop(0, 20)
    def _(i):
        rows = pl.ds(pl.multiple_of(i * 16, 16), 16)
        for b in range(8):
            cols = pl.ds(b * BLOCK, BLOCK)
            d = gl[rows, cols] - wl[rows, cols].astype(F32)
            s = (jnp.max(jnp.abs(d), axis=-1, keepdims=True) + 1e-06).astype(BF16).astype(F32)
            dec[rows, cols] = (d / s).astype(BF16).astype(F32) * s

    def quarter(q):
        return pl.ds(pl.multiple_of(q * 80, 16), 80)

    scatter = [
        remote(dec.at[quarter(lax.rem(x + j, 4))], rsb.at[j - 1], x_s.at[j - 1], x_r.at[j - 1], xdev[j - 1])
        for j in (1, 2, 3)
    ]
    for cp in scatter:
        cp.start()
    ysum = remote(ysend, yrecv, yl_s, yl_r, ydev)
    spread = [
        remote(mean.at[quarter(x)], mean.at[quarter(x)], xg_s.at[j - 1], xg_r.at[j - 1], xdev[j - 1])
        for j in (1, 2, 3)
    ]
    acc[...] = jnp.zeros_like(acc)

    def mm(h_col, w_ref, depth):
        for n in range(2):
            cols = pl.ds(n * 256, 256)
            acc[:, cols] += jnp.dot(
                H[:, pl.ds(pl.multiple_of(h_col, 128), depth)], w_ref[:, cols], preferred_element_type=F32
            )

    def mm_chunk(kind, half, slot):
        base = slot * 640
        if kind == "B":
            mm(r * 5120 + base + half * 256, chunk_ref(kind, half, slot), 256)
        elif half == 0:
            mm(r * 5120 + base + 512, chunk_ref(kind, half, slot), 128)
        else:
            mm((1 - r) * 5120 + base + 512, chunk_ref(kind, half, slot), 128)

    def mm_arrival(i):
        kind, half, dist = RING[i]
        if kind == "B":
            @pl.loop(0, 2)
            def _(way):
                slot = lax.rem(z + 8 + (2 * way - 1) * (dist + 1), 8)
                h_ = way if half == 0 else 1 - way
                mm(
                    r * 5120 + slot * 640 + h_ * 256,
                    WB.at[slot, pl.ds(pl.multiple_of(h_ * 256, 256), 256)], 256,
                )
        else:
            for way in range(2):
                mm_chunk(kind, half if way == 0 else 1 - half, slot_of(way, dist + 1))

    def mean_squares(part):
        @pl.loop(0, 4)
        def _(k):
            rows = pl.ds(pl.multiple_of(part * 256 + k * 64, 64), 64)

            def body(k, total):
                for s in range(4):
                    v = H[rows, pl.ds(pl.multiple_of(k * 512 + s * 128, 128), 128)].astype(F32)
                    total = total + v * v
                return total

            total = lax.fori_loop(0, 20, body, jnp.zeros((64, 128), F32))
            ms = jnp.sum(total, axis=-1, keepdims=True) * (1.0 / 10240)
            inv[rows, :] = jnp.broadcast_to(lax.rsqrt(ms + 1e-05) * (1.0 / math.sqrt(10240)), (64, 128))

    def partner_mm(g, slot, first=False):
        left = HP[g, :, pl.ds(pl.multiple_of(slot * 512, 512), 512)]
        for n in range(2):
            cols = pl.ds(n * 256, 256)
            part = jnp.dot(left, WB[slot, pl.ds(0, 512), cols], preferred_element_type=F32)
            accp[:, cols] = part if first else accp[:, cols] + part

    back = [
        [
            remote(
                PS.at[g, pl.ds(pl.multiple_of(core * 128, 128), 128)],
                PR.at[g, pl.ds(pl.multiple_of(core * 128, 128), 128)],
                yp_s.at[g, k], yp_r.at[g, k], partner,
            )
            for k, core in enumerate((o, c))
        ]
        for g in range(2)
    ]

    def send_back(g):
        PS[g] = accp[...].astype(BF16)
        for cp in back[g]:
            cp.start()


    def take_relay(q):
        for cp in groups[q]:
            cp.wait_recv()
        relays[q].start()

    for i in range(N_RING):
        for way in range(2):
            ring[way][i].wait_recv()
            if i + 2 < N_RING:
                if i == 2 and way == 0:
                    cross.wait_recv()
                ring[way][i + 2].start()
        send_hidden(HID_NEXT[i])
        for q in range(4):
            if RELAY_AT[q] == i:
                take_relay(q)
        if i == 2:
            for cp in h_sib:
                cp.wait_recv()
            for half in range(2):
                mm_chunk("B", half, z)
                mm_chunk("A", half, z)
            for k in range(3):
                mm_arrival(k)
            for cp in scatter:
                cp.wait_recv()
            for k in range(5):
                rows = pl.ds(k * 16, 16)
                own = dec[pl.ds(pl.multiple_of(x * 80 + k * 16, 16), 16), :]
                ysend[rows, :] = (own + rsb[0, rows, :] + rsb[1, rows, :] + rsb[2, rows, :]).astype(BF16)
            ysum.start()
        elif i > 2:
            mm_arrival(i)
        if i == 0:
            h_sib[2].start()
            h_sib[3].start()
            l_h.wait()
            mean_squares(c)
        if i == 3:
            mean_squares(o)
        if i == 5:
            ysum.wait_recv()
            for k in range(5):
                rows = pl.ds(k * 16, 16)
                mean[pl.ds(pl.multiple_of(x * 80 + k * 16, 16), 16), :] = (
                    ysend[rows, :].astype(F32) + yrecv[rows, :].astype(F32)
                ) * 0.125
            for cp in spread:
                cp.start()
        if i == SUM_AT[0] - 2:
            relays[0].wait_recv()
            relays[1].wait_recv()
            partner_mm(0, z, first=True)

            @pl.loop(0, 4)
            def _(k):
                partner_mm(0, lax.rem(z + jnp.where(k < 2, k + 1, k + 4), 8))

        if i == SUM_AT[0] - 1:
            @pl.loop(0, 2)
            def _(k):
                partner_mm(0, lax.rem(z + 3 + 2 * k, 8))

        if i == SUM_AT[0]:
            partner_mm(0, lax.rem(z + 4, 8))
            send_back(0)
            relays[2].wait_recv()
            partner_mm(1, 0, first=True)

            @pl.loop(1, 4)
            def _(k):
                partner_mm(1, k)

        if i == STATE_AT:
            for cp in spread:
                cp.wait_recv()
            l_m.wait()

            @pl.loop(0, 20)
            def _(k):
                rows = pl.ds(pl.multiple_of(k * 16, 16), 16)
                md = mean[rows, :]
                new_m = 0.9 * mo[rows, :] + md
                nm[rows, :] = new_m
                ng[rows, :] = gl[rows, :] - 0.7 * (0.9 * new_m + md)

            o_m = pltpu.make_async_copy(nm, nm_out, loc.at[5])
            o_g = pltpu.make_async_copy(ng, ng_out, loc.at[6])
            o_m.start()
            o_g.start()
        if i == SUM_AT[1]:
            relays[3].wait_recv()

            @pl.loop(4, 8)
            def _(k):
                partner_mm(1, k)

            send_back(1)

    def finish(core, g):
        rows = pl.ds(pl.multiple_of(core * 256 + g * 128, 128), 128)
        total = acc[rows, :] + PR[g, pl.ds(pl.multiple_of(core * 128, 128), 128), :].astype(F32)
        return (total * inv[rows, :][:, :1]).astype(BF16)

    o_k = [
        pltpu.make_async_copy(
            KO.at[pl.ds(g * 128, 128)], keys_out.at[pl.ds(g * 128, 128), own_cols], loc.at[7 + g]
        )
        for g in range(2)
    ]
    swap = [
        remote(
            KS.at[pl.ds(g * 128, 128)], keys_out.at[pl.ds(g * 128, 128), own_cols], sib_s.at[2 + g], sib_r.at[2 + g], sib
        )
        for g in range(2)
    ]
    for g in range(2):
        back[g][0].wait_recv()
        KS[pl.ds(g * 128, 128), :] = finish(o, g)
        swap[g].start()
        back[g][1].wait_recv()
        KO[pl.ds(g * 128, 128), :] = finish(c, g)
        o_k[g].start()
    for g in range(2):
        swap[g].wait_recv()

    w_sib.wait_send()
    for cp in h_sib:
        cp.wait_send()
    cross.wait_send()
    ysum.wait_send()
    for cp in [cp for grp in groups for cp in grp] + relays + ring[0] + ring[1] + back[0] + back[1] + scatter + spread + swap:
        cp.wait_send()
    o_m.wait()
    o_g.wait()
    o_k[0].wait()
    o_k[1].wait()


def write_out(a, b, c, a_out, b_out, c_out, sems):
    copies = [
        pltpu.make_async_copy(src, dst, sems.at[i])
        for i, (src, dst) in enumerate(((a, a_out), (b, b_out), (c, c_out)))
    ]
    for cp in copies:
        cp.start()
    for cp in copies:
        cp.wait()


def shards(hidden, norm_gain, local_weight, global_weight, momentum):
    weight_rows = local_weight[0]
    dma = pltpu.SemaphoreType.DMA
    V = pltpu.VMEM
    parts = tuple(pl.pallas_call(
        kernel,
        out_shape=(
            jax.ShapeDtypeStruct((256, 1024), BF16),
            jax.ShapeDtypeStruct((320, 1024), F32),
            jax.ShapeDtypeStruct((320, 1024), F32),
        ),
        in_specs=[pl.BlockSpec(memory_space=pl.ANY)] * 5,
        out_specs=(pl.BlockSpec(memory_space=pl.ANY),) * 3,
        scratch_shapes=[
            V((80, 128), F32), V((320, 512), BF16), V((512, 10240), BF16), V((2, 256, 4096), BF16), V((8, 640, 512), BF16), V((8, 128, 512), BF16),
            V((512, 512), F32), V((256, 512), F32), V((2, 256, 512), BF16), V((2, 256, 512), BF16),
            V((320, 1024), BF16), V((320, 1024), F32), V((320, 1024), F32), V((320, 1024), F32),
            V((3, 80, 1024), F32), V((80, 1024), BF16), V((80, 1024), BF16), V((320, 1024), F32),
            V((320, 1024), F32), V((320, 1024), F32), V((512, 128), F32), V((256, 512), BF16), V((256, 512), BF16),
            dma((9,)), dma((4,)), dma((4,)), dma((4,)), dma((4,)), dma((4,)), dma((4,)), dma((2, N_RING)), dma((2, N_RING)),
            dma, dma, dma((4, 4)), dma((4, 4)), dma((2, 2)), dma((2, 2)), dma((3,)), dma((3,)), dma((3,)), dma((3,)),
            dma, dma,
        ],
        compiler_params=pltpu.CompilerParams(
            collective_id=0, has_side_effects=True, vmem_limit_bytes=50 * 1024 * 1024
        ),
        cost_estimate=pl.CostEstimate(flops=5368709120, bytes_accessed=12000000, transcendentals=512),
    )(pltpu.with_memory_space_constraint(norm_gain.reshape(80, 128), pltpu.HBM), hidden, pltpu.with_memory_space_constraint(weight_rows, pltpu.HBM), global_weight, momentum))
    return tuple(pl.pallas_call(
        write_out,
        out_shape=tuple(jax.ShapeDtypeStruct(part.shape, part.dtype) for part in parts),
        in_specs=[pl.BlockSpec(memory_space=pltpu.VMEM)] * 3,
        out_specs=(pl.BlockSpec(memory_space=pl.ANY),) * 3,
        scratch_shapes=[dma((3,))],
        compiler_params=pltpu.CompilerParams(vmem_limit_bytes=8 * 1024 * 1024),
    )(*parts))


def solution(mesh):
    return jax.shard_map(
        shards,
        mesh=mesh,
        in_specs=(
            P(("replica", "fsdp"), None),
            P(),
            P("replica", "fsdp", None),
            P("fsdp", None),
            P("fsdp", None),
        ),
        out_specs=(P(("replica", "fsdp"), None), P("fsdp", None), P("fsdp", None)),
        check_vma=False,
    )
```
